32 devices in a mesh: groups: 2 (over y), seq: 16 (over z, x, core).
Axes of the slice: x: 2, y: 2, z: 4, core: 2. Of those that a mesh axis runs over, the one named last changes fastest.
Arguments:
- queries: bfloat16 [4, 128, 128, 128], P('groups', 'seq'), parts along dimension 0, may hold values from -64 to 64
- new_k: bfloat16 [4, 128, 8, 128], P('groups', 'seq'), parts along dimension 0, may hold values from -15 to 15
- new_v: bfloat16 [4, 128, 8, 128], P('groups', 'seq'), parts along dimension 0, may hold values from -6 to 6
- cache_k: bfloat16 [4, 8192, 8, 128], P('groups', 'seq'), parts along dimension 0, may hold values from -12 to 12
- cache_v: bfloat16 [4, 8192, 8, 128], P('groups', 'seq'), parts along dimension 0, may hold values from -6 to 6
- cache_len: int32 [4], P('groups'), parts along dimension 0, may hold values from 2048 to 8192
Outputs:
- attended: bfloat16 [4, 128, 128, 128], P('groups', 'seq'), parts along dimension 0
The draws below stay inside these ranges and needn't reach their ends.
There are 2 independent parts, one for each index of `groups`. The reference program is written for one: setup_inputs(seed, part) draws one part's arguments, and reference() takes and returns one part's arrays. A program takes and returns all parts, laid end to end along the dimension named above; each array names one. Nothing has to cross between parts.
Inputs may be any that keep to these rules, and one draw needn't show every extreme that they name: The first cache_len[r] of the 8192 cache slots of request r hold keys and values; the rest are to be ignored.
All inputs are finite; a program needn't handle non-finite values.
Results may differ from the reference program's by a relative error of at most 0.004.
Values may be sent and summed in bfloat16 or wider, within the bound.
A program may use at most 128 MiB of HBM per device.

```python
import math
import jax
import jax.numpy as jnp
from jax import lax

H = 128
KVH = 8
HD = 128
REQS = 2
NEW = 128
CTX_DEV = 512
CTX = 8192
N_SEQ = 16


def attention_field(key):
    seeded = jax.random.fold_in(key, 7)
    key_field = 2.0 * jnp.clip(jax.random.normal(jax.random.fold_in(seeded, 1), (REQS, CTX, KVH, HD), jnp.float32), -6.0, 6.0)
    query_field = 2.0 * jnp.clip(jax.random.normal(jax.random.fold_in(seeded, 2), (REQS, NEW, H, HD), jnp.float32), -6.0, 6.0)
    return (key_field, query_field)


def draw_queries(key, part):
    return attention_field(key)[1].astype(jnp.bfloat16)


def draw_cache_k(key, part):
    return attention_field(key)[0].astype(jnp.bfloat16)


def block_scale(key, dims, shards, smallest, top_value):
    def one(dim, shards_of):
        steps = jax.random.uniform(jax.random.fold_in(jax.random.fold_in(key, 6), dim), (shards_of,), jnp.float32, smallest / len(shards), top_value / len(shards))
        return jnp.repeat(jnp.exp(steps), dims[dim] // shards_of).reshape((-1,) + (1,) * (len(dims) - dim - 1))

    gain = one(*shards[0])
    for cut in shards[1:]:
        gain = gain * one(*cut)
    return gain


def centred(key, extent, scale, limit, pieces=(), held_as=jnp.bfloat16):
    result = scale * jax.random.normal(key, extent, jnp.float32)
    if pieces:
        result = result * block_scale(key, extent, pieces, -0.22, 0.18)
    return jnp.clip(result, -limit, limit).astype(held_as)


def setup_inputs(seed: int = 0, part: int = 0) -> dict:
    key_of = jax.random.split(jax.random.key(seed), 7)
    own_keys = jax.random.split(jax.random.fold_in(key_of[6], part), 7)
    return {
        "queries": draw_queries(jax.random.fold_in(jax.random.fold_in(key_of[6], part), 71), part),
        "new_k": centred(own_keys[1], (REQS, NEW, KVH, HD), 2.5, 15.0, ((1, 16),)),
        "new_v": centred(own_keys[2], (REQS, NEW, KVH, HD), 1.0, 6.0, ((1, 16),)),
        "cache_k": draw_cache_k(jax.random.fold_in(jax.random.fold_in(key_of[6], part), 71), part),
        "cache_v": centred(own_keys[4], (REQS, CTX, KVH, HD), 1.0, 6.0, ((1, 16),)),
        "cache_len": jax.random.randint(own_keys[5], (REQS,), CTX // 4, CTX + 1).astype(jnp.int32),
    }


def reference(queries, new_k, new_v, cache_k, cache_v, cache_len):
    group_size = H // KVH
    scaling = 1.0 / math.sqrt(HD)
    query_f32 = queries.astype(jnp.float32).reshape(REQS, NEW, KVH, group_size, HD)
    key_blocks = jnp.moveaxis(cache_k.reshape(REQS, N_SEQ, CTX_DEV, KVH, HD), 1, 0)
    value_blocks = jnp.moveaxis(cache_v.reshape(REQS, N_SEQ, CTX_DEV, KVH, HD), 1, 0)

    def absorb(state, scores, valid, values):
        row_max, row_sum, partial_value = state
        scores = jnp.where(valid, scores, -1e+30)
        new_max = jnp.maximum(row_max, lax.optimization_barrier(jnp.max(scores, axis=-1)))
        weights = jnp.where(valid, jnp.exp(scores - new_max[..., None]), 0.0)
        rescale = jnp.exp(row_max - new_max)
        row_sum = row_sum * rescale + lax.optimization_barrier(jnp.sum(weights, axis=-1))
        rounded = weights.astype(jnp.bfloat16).astype(jnp.float32)
        partial_value = partial_value * rescale[..., None] + jnp.einsum('rnkgc,rckd->rnkgd', rounded, values.astype(jnp.float32))
        return (new_max, row_sum, partial_value)

    def step(state, inputs):
        key_block, value_block, block_index = inputs
        scores = jnp.einsum('rnkgd,rckd->rnkgc', query_f32, key_block.astype(jnp.float32)) * scaling
        slot_pos = block_index * CTX_DEV + jnp.arange(CTX_DEV, dtype=jnp.int32)
        valid = (slot_pos[None, :] < cache_len[:, None])[:, None, None, None, :]
        return (absorb(state, scores, valid, value_block), None)
    start_state = (jnp.full((REQS, NEW, KVH, group_size), -1e+30, jnp.float32), jnp.zeros((REQS, NEW, KVH, group_size), jnp.float32), jnp.zeros((REQS, NEW, KVH, group_size, HD), jnp.float32))
    state, _ = lax.scan(step, start_state, (key_blocks, value_blocks, jnp.arange(N_SEQ, dtype=jnp.int32)))
    fresh_scores = jnp.einsum('rnkgd,rukd->rnkgu', query_f32, new_k.astype(jnp.float32)) * scaling
    positions = jnp.arange(NEW, dtype=jnp.int32)
    fresh_valid = (positions[None, :] <= positions[:, None])[None, :, None, None, :]
    row_max, row_sum, partial_value = absorb(state, fresh_scores, fresh_valid, new_v)
    merged = partial_value / row_sum[..., None]
    return merged.reshape(REQS, NEW, H, HD).astype(jnp.bfloat16)
```

```python
import functools
import math

import jax
import jax.numpy as jnp
from jax import lax
from jax.experimental import pallas as pl
from jax.experimental.pallas import tpu as pltpu
from jax.sharding import PartitionSpec as P

MESH = pl.DeviceIdType.MESH
LOW = -1e30


def loop(start, stop, body):
    def step(i, carry):
        body(i)
        return carry

    lax.fori_loop(start, stop, step, jnp.int32(0))


def kernel(
    n, heads, requests, slots, local_rows, group, owners, span,
    len_ref, q_ref, new_ref, k_ref, v_ref, out_ref,
    all_q, all_new, all_k, all_v, part, stat, got, got_stat,
    own_sem, q_send, q_recv, new_send, new_recv, k_send, k_recv, v_send, v_recv,
    o_send, o_recv, s_send, s_recv,
):
    me = lax.axis_index("seq")
    block = me // heads
    my_head = lax.rem(me, heads)
    base = block * heads
    blocks = n // heads
    rows = local_rows * group
    padded = all_new.shape[3]
    head_dim = q_ref.shape[-1]
    factor = math.log2(math.e) / math.sqrt(head_dim)

    barrier = pltpu.get_barrier_semaphore()
    loop(1, n, lambda i: pl.semaphore_signal(
        barrier, inc=1, device_id={"seq": lax.rem(me + i, n)}, device_id_type=MESH))
    pl.semaphore_wait(barrier, n - 1)

    def remote(src, dst, send, recv, device):
        return pltpu.make_async_remote_copy(
            src_ref=src, dst_ref=dst, send_sem=send, recv_sem=recv,
            device_id={"seq": device}, device_id_type=MESH)

    def q_copy(device, source):
        return remote(q_ref.at[lax.rem(device, heads)], all_q.at[:, source],
                      q_send.at[device], q_recv.at[source], device)

    def new_copy(j, source):
        return remote(new_ref.at[j], all_new.at[:, :, source],
                      new_send.at[j], new_recv.at[source], base + j)

    def k_copy(r, j, source):
        return remote(k_ref.at[j, r], all_k.at[r, source],
                      k_send.at[r, j], k_recv.at[r, source], base + j)

    def v_copy(r, j, source):
        return remote(v_ref.at[j, r], all_v.at[r, source],
                      v_send.at[r, j], v_recv.at[r, source], base + j)

    def o_copy(r, device, source):
        return remote(part.at[r, device], got.at[r, source],
                      o_send.at[r, device], o_recv.at[r, source], device)

    def s_copy(r, device, source):
        return remote(stat.at[r, device], got_stat.at[r, source],
                      s_send.at[r, device], s_recv.at[r, source], device)

    other = lambda i: lax.rem(me + i, n)
    peer = lambda i: lax.rem(my_head + i, heads)

    loop(1, n, lambda i: q_copy(other(i), me).start())
    loop(1, heads, lambda i: new_copy(peer(i), my_head).start())
    for r in range(requests):
        loop(1, heads, lambda i: k_copy(r, peer(i), my_head).start())
        loop(1, heads, lambda i: v_copy(r, peer(i), my_head).start())

    own = [
        pltpu.make_async_copy(q_ref.at[my_head], all_q.at[:, me], own_sem.at[0]),
        pltpu.make_async_copy(new_ref.at[my_head], all_new.at[:, :, my_head], own_sem.at[1]),
    ]
    for r in range(requests):
        own.append(pltpu.make_async_copy(
            k_ref.at[my_head, r], all_k.at[r, my_head], own_sem.at[2 + 2 * r]))
        own.append(pltpu.make_async_copy(
            v_ref.at[my_head, r], all_v.at[r, my_head], own_sem.at[3 + 2 * r]))
    for copy in own:
        copy.start()
    for copy in own:
        copy.wait()

    loop(1, n, lambda i: q_copy(me, other(i)).wait_recv())
    loop(1, heads, lambda i: new_copy(my_head, peer(i)).wait_recv())

    step_rows = owners * rows
    steps = n // owners
    for r in range(requests):
        loop(1, heads, lambda i: k_copy(r, my_head, peer(i)).wait_recv())
        loop(1, heads, lambda i: v_copy(r, my_head, peer(i)).wait_recv())
        filled = len_ref[r]

        def attend(i, r=r, filled=filled):
            step = lax.rem(i + me, steps)
            first = step * owners
            q = all_q[r, pl.ds(first, owners)].reshape(step_rows, head_dim)

            def absorb(state, scores, values):
                peak, total, value = state
                new_peak = jnp.maximum(peak, jnp.max(scores, axis=1, keepdims=True))
                rescale = jnp.exp2(peak - new_peak)
                weights = jnp.exp2(scores - new_peak)
                total = total * rescale + jnp.sum(weights, axis=1, keepdims=True)
                value = value * rescale + jnp.dot(
                    weights.astype(jnp.bfloat16), values, preferred_element_type=jnp.float32)
                return new_peak, total, value

            def score(keys):
                return lax.dot_general(
                    q, keys, (((1,), (1,)), ((), ())),
                    preferred_element_type=jnp.float32) * factor

            state = (
                jnp.full((step_rows, 1), LOW, jnp.float32),
                jnp.zeros((step_rows, 1), jnp.float32),
                jnp.zeros((step_rows, head_dim), jnp.float32),
            )
            for c in range(0, heads, span):
                keys = all_k[r, c:c + span].reshape(span * slots, head_dim)
                values = all_v[r, c:c + span].reshape(span * slots, head_dim)
                pos = (base + c) * slots + lax.broadcasted_iota(
                    jnp.int32, (1, span * slots), 1)
                bias = jnp.where(pos < filled, 0.0, LOW)
                state = absorb(state, score(keys) + bias, values)
            width = heads * padded
            keys = all_new[r, 0].reshape(width, head_dim)
            values = all_new[r, 1].reshape(width, head_dim)
            lane = lax.broadcasted_iota(jnp.int32, (step_rows, width), 1)
            row = lax.broadcasted_iota(jnp.int32, (step_rows, width), 0)
            inner = lax.rem(lane, padded)
            key_pos = (base + lax.div(lane, padded)) * local_rows + inner
            row_pos = first * local_rows + lax.div(row, group)
            valid = (inner < local_rows) & (key_pos <= row_pos)
            peak, total, value = absorb(
                state, jnp.where(valid, score(keys), LOW), values)

            result = (value / total).astype(jnp.bfloat16).reshape(owners, rows, head_dim)
            lanes = lax.broadcasted_iota(jnp.int32, (step_rows, 128), 1)
            turned = jnp.where(lanes == 0, peak, total).T[:8]
            part[r, pl.ds(first, owners)] = result
            for j in range(owners):
                stat[r, first + j] = turned[:, j * rows:(j + 1) * rows]
            for j in range(owners):
                owner = first + j

                @pl.when(owner != me)
                def _():
                    o_copy(r, owner, me).start()
                    s_copy(r, owner, me).start()

                @pl.when(owner == me)
                def _():
                    got[r, owner] = result[j]
                    got_stat[r, owner] = turned[:, j * rows:(j + 1) * rows]

        loop(0, steps, attend)

    for r in range(requests):
        def arrive(i, r=r):
            o_copy(r, me, other(i)).wait_recv()
            s_copy(r, me, other(i)).wait_recv()

        loop(1, n, arrive)

        def merge(k, r=r):
            stats = [got_stat[r, b * heads + k] for b in range(blocks)]
            top = functools.reduce(jnp.maximum, [s[0:1] for s in stats])
            shares = [s[1:2] * jnp.exp2(s[0:1] - top) for s in stats]
            whole = functools.reduce(jnp.add, shares)
            shares = jnp.concatenate([s / whole for s in shares], axis=0)
            fill = -blocks % 128
            shares = jnp.concatenate(
                [shares, jnp.zeros((fill, rows), jnp.float32)], axis=0).T
            merged = functools.reduce(jnp.add, [
                shares[:, b:b + 1] * got[r, b * heads + k].astype(jnp.float32)
                for b in range(blocks)])
            merged = merged.astype(jnp.bfloat16).reshape(local_rows, group, head_dim)
            out_ref[r, :, pl.ds(pl.multiple_of(k * group, group), group), :] = merged

        loop(0, heads, merge)

    loop(1, n, lambda i: q_copy(other(i), me).wait_send())
    loop(1, heads, lambda i: new_copy(peer(i), my_head).wait_send())
    for r in range(requests):
        def leave(i, r=r):
            k_copy(r, peer(i), my_head).wait_send()
            v_copy(r, peer(i), my_head).wait_send()

        loop(1, heads, leave)

        def leave_out(i, r=r):
            o_copy(r, other(i), me).wait_send()
            s_copy(r, other(i), me).wait_send()

        loop(1, n, leave_out)


def shards(queries, new_k, new_v, cache_k, cache_v, cache_len):
    requests, local_rows, q_heads, head_dim = queries.shape
    slots, heads = cache_k.shape[1:3]
    group = q_heads // heads
    n = lax.axis_size("seq")
    rows = local_rows * group
    padded = -(-local_rows // 16) * 16
    owners = max(w for w in range(1, n + 1) if n % w == 0 and w * rows <= max(256, rows))
    span = max(w for w in range(1, heads + 1) if heads % w == 0 and w * slots <= max(1024, slots))

    q = jnp.transpose(
        queries.reshape(requests, local_rows, heads, group, head_dim), (2, 0, 1, 3, 4)
    ).reshape(heads, requests, rows, head_dim)
    new = jnp.transpose(jnp.stack([new_k, new_v]), (3, 1, 0, 2, 4))
    new = jnp.pad(new, ((0, 0), (0, 0), (0, 0), (0, padded - local_rows), (0, 0)))
    k = jnp.transpose(cache_k, (2, 0, 1, 3))
    v = jnp.transpose(cache_v, (2, 0, 1, 3))

    bf16, f32, dma = jnp.bfloat16, jnp.float32, pltpu.SemaphoreType.DMA
    scratch = [
        pltpu.VMEM((requests, n, rows, head_dim), bf16),
        pltpu.VMEM((requests, 2, heads, padded, head_dim), bf16),
        pltpu.VMEM((requests, heads, slots, head_dim), bf16),
        pltpu.VMEM((requests, heads, slots, head_dim), bf16),
        pltpu.VMEM((requests, n, rows, head_dim), bf16),
        pltpu.VMEM((requests, n, 8, rows), f32),
        pltpu.VMEM((requests, n, rows, head_dim), bf16),
        pltpu.VMEM((requests, n, 8, rows), f32),
        dma((2 + 2 * requests,)),
        dma((n,)), dma((n,)), dma((heads,)), dma((heads,)),
        dma((requests, heads)), dma((requests, heads)),
        dma((requests, heads)), dma((requests, heads)),
        dma((requests, n)), dma((requests, n)), dma((requests, n)), dma((requests, n)),
    ]
    work = requests * n * rows * heads * slots
    vmem = pl.BlockSpec(memory_space=pltpu.VMEM)
    return pl.pallas_call(
        functools.partial(
            kernel, n, heads, requests, slots, local_rows, group, owners, span),
        out_shape=jax.ShapeDtypeStruct(queries.shape, bf16),
        in_specs=[pl.BlockSpec(memory_space=pltpu.SMEM)] + [vmem] * 4,
        out_specs=vmem,
        scratch_shapes=scratch,
        compiler_params=pltpu.CompilerParams(
            collective_id=0, has_side_effects=True, vmem_limit_bytes=52 * 1024 * 1024),
        cost_estimate=pl.CostEstimate(
            flops=4 * work * head_dim, bytes_accessed=4 * k.size, transcendentals=work),
    )(cache_len, q, new, k, v)


def solution(mesh):
    spec = P("groups", "seq", None, None)
    in_specs = (spec, spec, spec, spec, spec, P("groups"))
    return jax.shard_map(
        shards, mesh=mesh, in_specs=in_specs, out_specs=spec, check_vma=False)
```

```python
import functools
import math

import jax
import jax.numpy as jnp
from jax import lax
from jax.experimental import pallas as pl
from jax.experimental.pallas import tpu as pltpu
from jax.sharding import PartitionSpec as P

MESH = pl.DeviceIdType.MESH
LOW = -1e30


def loop(start, stop, body):
    def step(i, carry):
        body(i)
        return carry

    lax.fori_loop(start, stop, step, jnp.int32(0))


def kernel(
    n, heads, requests, slots, local_rows, group, owners, span,
    len_ref, q_ref, new_ref, k_ref, v_ref, out_ref,
    all_q, all_new, all_k, all_v, part, stat, got, got_stat,
    own_sem, q_send, q_recv, new_send, new_recv, k_send, k_recv, v_send, v_recv,
    o_send, o_recv, s_send, s_recv,
):
    me = lax.axis_index("seq")
    block = me // heads
    my_head = lax.rem(me, heads)
    base = block * heads
    blocks = n // heads
    rows = local_rows * group
    padded = all_new.shape[3]
    head_dim = q_ref.shape[-1]
    factor = math.log2(math.e) / math.sqrt(head_dim)

    barrier = pltpu.get_barrier_semaphore()
    loop(1, n, lambda i: pl.semaphore_signal(
        barrier, inc=1, device_id={"seq": lax.rem(me + i, n)}, device_id_type=MESH))
    pl.semaphore_wait(barrier, n - 1)

    def remote(src, dst, send, recv, device):
        return pltpu.make_async_remote_copy(
            src_ref=src, dst_ref=dst, send_sem=send, recv_sem=recv,
            device_id={"seq": device}, device_id_type=MESH)

    def q_copy(device, source):
        return remote(q_ref.at[lax.rem(device, heads)], all_q.at[:, source],
                      q_send.at[device], q_recv.at[source], device)

    def new_copy(j, source):
        return remote(new_ref.at[j], all_new.at[:, :, source],
                      new_send.at[j], new_recv.at[source], base + j)

    def k_copy(r, j, source):
        return remote(k_ref.at[j, r], all_k.at[r, source],
                      k_send.at[r, j], k_recv.at[r, source], base + j)

    def v_copy(r, j, source):
        return remote(v_ref.at[j, r], all_v.at[r, source],
                      v_send.at[r, j], v_recv.at[r, source], base + j)

    def o_copy(r, device, source):
        return remote(part.at[r, device], got.at[r, source],
                      o_send.at[r, device], o_recv.at[r, source], device)

    def s_copy(r, device, source):
        return remote(stat.at[r, device], got_stat.at[r, source],
                      s_send.at[r, device], s_recv.at[r, source], device)

    other = lambda i: lax.rem(me + i, n)
    peer = lambda i: lax.rem(my_head + i, heads)

    loop(1, n, lambda i: q_copy(other(i), me).start())
    loop(1, heads, lambda i: new_copy(peer(i), my_head).start())
    for r in range(requests):
        loop(1, heads, lambda i: k_copy(r, peer(i), my_head).start())
        loop(1, heads, lambda i: v_copy(r, peer(i), my_head).start())

    own = [
        pltpu.make_async_copy(q_ref.at[my_head], all_q.at[:, me], own_sem.at[0]),
        pltpu.make_async_copy(new_ref.at[my_head], all_new.at[:, :, my_head], own_sem.at[1]),
    ]
    for r in range(requests):
        own.append(pltpu.make_async_copy(
            k_ref.at[my_head, r], all_k.at[r, my_head], own_sem.at[2 + 2 * r]))
        own.append(pltpu.make_async_copy(
            v_ref.at[my_head, r], all_v.at[r, my_head], own_sem.at[3 + 2 * r]))
    for copy in own:
        copy.start()
    for copy in own:
        copy.wait()

    loop(1, n, lambda i: q_copy(me, other(i)).wait_recv())
    loop(1, heads, lambda i: new_copy(my_head, peer(i)).wait_recv())

    step_rows = owners * rows
    steps = n // owners
    for r in range(requests):
        loop(1, heads, lambda i: k_copy(r, my_head, peer(i)).wait_recv())
        loop(1, heads, lambda i: v_copy(r, my_head, peer(i)).wait_recv())
        filled = len_ref[r]

        def attend(i, r=r, filled=filled):
            step = lax.rem(i + me, steps)
            first = step * owners
            q = all_q[r, pl.ds(first, owners)].reshape(step_rows, head_dim)

            def absorb(state, scores, values):
                peak, total, value = state
                new_peak = jnp.maximum(peak, jnp.max(scores, axis=1, keepdims=True))
                rescale = jnp.exp2(peak - new_peak)
                weights = jnp.exp2(scores - new_peak)
                total = total * rescale + jnp.sum(weights, axis=1, keepdims=True)
                value = value * rescale + jnp.dot(
                    weights.astype(jnp.bfloat16), values, preferred_element_type=jnp.float32)
                return new_peak, total, value

            def score(keys):
                return lax.dot_general(
                    q, keys, (((1,), (1,)), ((), ())),
                    preferred_element_type=jnp.float32) * factor

            state = (
                jnp.full((step_rows, 1), LOW, jnp.float32),
                jnp.zeros((step_rows, 1), jnp.float32),
                jnp.zeros((step_rows, head_dim), jnp.float32),
            )
            for c in range(0, heads, span):
                keys = all_k[r, c:c + span].reshape(span * slots, head_dim)
                values = all_v[r, c:c + span].reshape(span * slots, head_dim)
                pos = (base + c) * slots + lax.broadcasted_iota(
                    jnp.int32, (1, span * slots), 1)
                bias = jnp.where(pos < filled, 0.0, LOW)
                state = absorb(state, score(keys) + bias, values)
            width = heads * padded
            keys = all_new[r, 0].reshape(width, head_dim)
            values = all_new[r, 1].reshape(width, head_dim)
            lane = lax.broadcasted_iota(jnp.int32, (step_rows, width), 1)
            row = lax.broadcasted_iota(jnp.int32, (step_rows, width), 0)
            inner = lax.rem(lane, padded)
            key_pos = (base + lax.div(lane, padded)) * local_rows + inner
            row_pos = first * local_rows + lax.div(row, group)
            valid = (inner < local_rows) & (key_pos <= row_pos)
            peak, total, value = absorb(
                state, jnp.where(valid, score(keys), LOW), values)

            result = (value * (1.0 / total)).astype(jnp.bfloat16).reshape(owners, rows, head_dim)
            lanes = lax.broadcasted_iota(jnp.int32, (step_rows, 128), 1)
            turned = jnp.where(lanes == 0, peak, total).T[:8]
            part[r, pl.ds(first, owners)] = result
            for j in range(owners):
                stat[r, first + j] = turned[:, j * rows:(j + 1) * rows]
            for j in range(owners):
                owner = first + j

                @pl.when(owner != me)
                def _():
                    o_copy(r, owner, me).start()
                    s_copy(r, owner, me).start()

                @pl.when(owner == me)
                def _():
                    got[r, owner] = result[j]
                    got_stat[r, owner] = turned[:, j * rows:(j + 1) * rows]

        loop(0, steps, attend)

    for r in range(requests):
        def arrive(i, r=r):
            o_copy(r, me, other(i)).wait_recv()
            s_copy(r, me, other(i)).wait_recv()

        loop(1, n, arrive)

        stats = [got_stat[r, b * heads:(b + 1) * heads] for b in range(blocks)]
        top = functools.reduce(jnp.maximum, [s[:, 0] for s in stats])
        shares = [s[:, 1] * jnp.exp2(s[:, 0] - top) for s in stats]
        whole = functools.reduce(jnp.add, shares)
        shares = [s / whole for s in shares]
        fill = -n % 128
        if fill:
            shares.append(jnp.zeros((fill, rows), jnp.float32))
        shares = jnp.concatenate(shares, axis=0).T
        for k in range(heads):
            merged = functools.reduce(jnp.add, [
                shares[:, b * heads + k:b * heads + k + 1]
                * got[r, b * heads + k].astype(jnp.float32)
                for b in range(blocks)])
            merged = merged.astype(jnp.bfloat16).reshape(local_rows, group, head_dim)
            out_ref[r, :, k * group:(k + 1) * group, :] = merged

    loop(1, n, lambda i: q_copy(other(i), me).wait_send())
    loop(1, heads, lambda i: new_copy(peer(i), my_head).wait_send())
    for r in range(requests):
        def leave(i, r=r):
            k_copy(r, peer(i), my_head).wait_send()
            v_copy(r, peer(i), my_head).wait_send()

        loop(1, heads, leave)

        def leave_out(i, r=r):
            o_copy(r, other(i), me).wait_send()
            s_copy(r, other(i), me).wait_send()

        loop(1, n, leave_out)


def shards(queries, new_k, new_v, cache_k, cache_v, cache_len):
    requests, local_rows, q_heads, head_dim = queries.shape
    slots, heads = cache_k.shape[1:3]
    group = q_heads // heads
    n = lax.axis_size("seq")
    rows = local_rows * group
    padded = -(-local_rows // 16) * 16
    owners = max(w for w in range(1, n + 1) if n % w == 0 and w * rows <= max(512, rows))
    span = max(w for w in range(1, heads + 1) if heads % w == 0 and w * slots <= max(1024, slots))

    q = jnp.transpose(
        queries.reshape(requests, local_rows, heads, group, head_dim), (2, 0, 1, 3, 4)
    ).reshape(heads, requests, rows, head_dim)
    new = jnp.transpose(jnp.stack([new_k, new_v]), (3, 1, 0, 2, 4))
    new = jnp.pad(new, ((0, 0), (0, 0), (0, 0), (0, padded - local_rows), (0, 0)))
    k = jnp.transpose(cache_k, (2, 0, 1, 3))
    v = jnp.transpose(cache_v, (2, 0, 1, 3))

    bf16, f32, dma = jnp.bfloat16, jnp.float32, pltpu.SemaphoreType.DMA
    scratch = [
        pltpu.VMEM((requests, n, rows, head_dim), bf16),
        pltpu.VMEM((requests, 2, heads, padded, head_dim), bf16),
        pltpu.VMEM((requests, heads, slots, head_dim), bf16),
        pltpu.VMEM((requests, heads, slots, head_dim), bf16),
        pltpu.VMEM((requests, n, rows, head_dim), bf16),
        pltpu.VMEM((requests, n, 8, rows), f32),
        pltpu.VMEM((requests, n, rows, head_dim), bf16),
        pltpu.VMEM((requests, n, 8, rows), f32),
        dma((2 + 2 * requests,)),
        dma((n,)), dma((n,)), dma((heads,)), dma((heads,)),
        dma((requests, heads)), dma((requests, heads)),
        dma((requests, heads)), dma((requests, heads)),
        dma((requests, n)), dma((requests, n)), dma((requests, n)), dma((requests, n)),
    ]
    work = requests * n * rows * heads * slots
    vmem = pl.BlockSpec(memory_space=pltpu.VMEM)
    return pl.pallas_call(
        functools.partial(
            kernel, n, heads, requests, slots, local_rows, group, owners, span),
        out_shape=jax.ShapeDtypeStruct(queries.shape, bf16),
        in_specs=[pl.BlockSpec(memory_space=pltpu.SMEM)] + [vmem] * 4,
        out_specs=vmem,
        scratch_shapes=scratch,
        compiler_params=pltpu.CompilerParams(
            collective_id=0, has_side_effects=True, vmem_limit_bytes=52 * 1024 * 1024),
        cost_estimate=pl.CostEstimate(
            flops=4 * work * head_dim, bytes_accessed=4 * k.size, transcendentals=work),
    )(cache_len, q, new, k, v)


def solution(mesh):
    spec = P("groups", "seq", None, None)
    in_specs = (spec, spec, spec, spec, spec, P("groups"))
    return jax.shard_map(
        shards, mesh=mesh, in_specs=in_specs, out_specs=spec, check_vma=False)
```

```python
import functools
import math

import jax
import jax.numpy as jnp
from jax import lax
from jax.experimental import pallas as pl
from jax.experimental.pallas import tpu as pltpu
from jax.sharding import PartitionSpec as P

MESH = pl.DeviceIdType.MESH
LOW = -1e30


def loop(start, stop, body):
    def step(i, carry):
        body(i)
        return carry

    lax.fori_loop(start, stop, step, jnp.int32(0))


def kernel(
    n, heads, requests, slots, local_rows, group, owners, span,
    len_ref, q_ref, new_ref, cache_k_ref, cache_v_ref, out_ref, k_ref, v_ref, wide,
    all_q, all_new, all_k, all_v, part, stat, got, got_stat,
    own_sem, q_send, q_recv, new_send, new_recv, k_send, k_recv, v_send, v_recv,
    o_send, o_recv, s_send, s_recv,
):
    me = lax.axis_index("seq")
    block = me // heads
    my_head = lax.rem(me, heads)
    base = block * heads
    blocks = n // heads
    rows = local_rows * group
    padded = all_new.shape[3]
    head_dim = q_ref.shape[-1]
    factor = math.log2(math.e) / math.sqrt(head_dim)

    barrier = pltpu.get_barrier_semaphore()
    loop(1, n, lambda i: pl.semaphore_signal(
        barrier, inc=1, device_id={"seq": lax.rem(me + i, n)}, device_id_type=MESH))
    pl.semaphore_wait(barrier, n - 1)

    def remote(src, dst, send, recv, device):
        return pltpu.make_async_remote_copy(
            src_ref=src, dst_ref=dst, send_sem=send, recv_sem=recv,
            device_id={"seq": device}, device_id_type=MESH)

    def q_copy(device, source):
        return remote(q_ref.at[lax.rem(device, heads)], all_q.at[:, source],
                      q_send.at[device], q_recv.at[source], device)

    def new_copy(j, source):
        return remote(new_ref.at[j], all_new.at[:, :, source],
                      new_send.at[j], new_recv.at[source], base + j)

    def k_copy(r, j, source):
        return remote(k_ref.at[j, r], all_k.at[r, source],
                      k_send.at[r, j], k_recv.at[r, source], base + j)

    def v_copy(r, j, source):
        return remote(v_ref.at[j, r], all_v.at[r, source],
                      v_send.at[r, j], v_recv.at[r, source], base + j)

    def o_copy(r, device, source):
        return remote(part.at[r, device], got.at[r, source],
                      o_send.at[r, device], o_recv.at[r, source], device)

    def s_copy(r, device, source):
        return remote(stat.at[r, device], got_stat.at[r, source],
                      s_send.at[r, device], s_recv.at[r, source], device)

    other = lambda i: lax.rem(me + i, n)
    peer = lambda i: lax.rem(my_head + i, heads)

    loop(1, n, lambda i: q_copy(other(i), me).start())
    loop(1, heads, lambda i: new_copy(peer(i), my_head).start())
    def turn(cache_ref, turned_ref, r):
        wide[...] = cache_ref[r].astype(jnp.float32).reshape(slots * heads, head_dim)
        for h in range(heads):
            turned_ref[h, r] = wide[pl.ds(h, slots, stride=heads), :].astype(jnp.bfloat16)

    for r in range(requests):
        turn(cache_k_ref, k_ref, r)
        loop(1, heads, lambda i: k_copy(r, peer(i), my_head).start())
        turn(cache_v_ref, v_ref, r)
        loop(1, heads, lambda i: v_copy(r, peer(i), my_head).start())

    own = [
        pltpu.make_async_copy(q_ref.at[my_head], all_q.at[:, me], own_sem.at[0]),
        pltpu.make_async_copy(new_ref.at[my_head], all_new.at[:, :, my_head], own_sem.at[1]),
    ]
    for r in range(requests):
        own.append(pltpu.make_async_copy(
            k_ref.at[my_head, r], all_k.at[r, my_head], own_sem.at[2 + 2 * r]))
        own.append(pltpu.make_async_copy(
            v_ref.at[my_head, r], all_v.at[r, my_head], own_sem.at[3 + 2 * r]))
    for copy in own:
        copy.start()
    for copy in own:
        copy.wait()

    loop(1, n, lambda i: q_copy(me, other(i)).wait_recv())
    loop(1, heads, lambda i: new_copy(my_head, peer(i)).wait_recv())

    step_rows = owners * rows
    steps = n // owners
    for r in range(requests):
        loop(1, heads, lambda i: k_copy(r, my_head, peer(i)).wait_recv())
        loop(1, heads, lambda i: v_copy(r, my_head, peer(i)).wait_recv())
        filled = len_ref[r]

        def attend(i, r=r, filled=filled):
            step = lax.rem(i + me, steps)
            first = step * owners
            q = all_q[r, pl.ds(first, owners)].reshape(step_rows, head_dim)

            def absorb(state, scores, values):
                peak, total, value = state
                new_peak = jnp.maximum(peak, jnp.max(scores, axis=1, keepdims=True))
                rescale = jnp.exp2(peak - new_peak)
                weights = jnp.exp2(scores - new_peak)
                total = total * rescale + jnp.sum(weights, axis=1, keepdims=True)
                value = value * rescale + jnp.dot(
                    weights.astype(jnp.bfloat16), values, preferred_element_type=jnp.float32)
                return new_peak, total, value

            def score(keys):
                return lax.dot_general(
                    q, keys, (((1,), (1,)), ((), ())),
                    preferred_element_type=jnp.float32) * factor

            state = (
                jnp.full((step_rows, 1), LOW, jnp.float32),
                jnp.zeros((step_rows, 1), jnp.float32),
                jnp.zeros((step_rows, head_dim), jnp.float32),
            )
            for c in range(0, heads, span):
                keys = all_k[r, c:c + span].reshape(span * slots, head_dim)
                values = all_v[r, c:c + span].reshape(span * slots, head_dim)
                pos = (base + c) * slots + lax.broadcasted_iota(
                    jnp.int32, (1, span * slots), 1)
                bias = jnp.where(pos < filled, 0.0, LOW)
                state = absorb(state, score(keys) + bias, values)
            width = heads * padded
            keys = all_new[r, 0].reshape(width, head_dim)
            values = all_new[r, 1].reshape(width, head_dim)
            lane = lax.broadcasted_iota(jnp.int32, (step_rows, width), 1)
            row = lax.broadcasted_iota(jnp.int32, (step_rows, width), 0)
            inner = lax.rem(lane, padded)
            key_pos = (base + lax.div(lane, padded)) * local_rows + inner
            row_pos = first * local_rows + lax.div(row, group)
            valid = (inner < local_rows) & (key_pos <= row_pos)
            peak, total, value = absorb(
                state, jnp.where(valid, score(keys), LOW), values)

            result = (value * (1.0 / total)).astype(jnp.bfloat16).reshape(owners, rows, head_dim)
            lanes = lax.broadcasted_iota(jnp.int32, (step_rows, 128), 1)
            turned = jnp.where(lanes == 0, peak, total).T[:8]
            part[r, pl.ds(first, owners)] = result
            for j in range(owners):
                stat[r, first + j] = turned[:, j * rows:(j + 1) * rows]
            for j in range(owners):
                owner = first + j

                @pl.when(owner != me)
                def _():
                    o_copy(r, owner, me).start()
                    s_copy(r, owner, me).start()

                @pl.when(owner == me)
                def _():
                    got[r, owner] = result[j]
                    got_stat[r, owner] = turned[:, j * rows:(j + 1) * rows]

        loop(0, steps, attend)

    for r in range(requests):
        def arrive(i, r=r):
            o_copy(r, me, other(i)).wait_recv()
            s_copy(r, me, other(i)).wait_recv()

        loop(1, n, arrive)

        stats = [got_stat[r, b * heads:(b + 1) * heads] for b in range(blocks)]
        top = functools.reduce(jnp.maximum, [s[:, 0] for s in stats])
        shares = [s[:, 1] * jnp.exp2(s[:, 0] - top) for s in stats]
        whole = functools.reduce(jnp.add, shares)
        shares = [s / whole for s in shares]
        fill = -n % 128
        if fill:
            shares.append(jnp.zeros((fill, rows), jnp.float32))
        shares = jnp.concatenate(shares, axis=0).T
        for k in range(heads):
            merged = functools.reduce(jnp.add, [
                shares[:, b * heads + k:b * heads + k + 1]
                * got[r, b * heads + k].astype(jnp.float32)
                for b in range(blocks)])
            merged = merged.astype(jnp.bfloat16).reshape(local_rows, group, head_dim)
            out_ref[r, :, k * group:(k + 1) * group, :] = merged

    loop(1, n, lambda i: q_copy(other(i), me).wait_send())
    loop(1, heads, lambda i: new_copy(peer(i), my_head).wait_send())
    for r in range(requests):
        def leave(i, r=r):
            k_copy(r, peer(i), my_head).wait_send()
            v_copy(r, peer(i), my_head).wait_send()

        loop(1, heads, leave)

        def leave_out(i, r=r):
            o_copy(r, other(i), me).wait_send()
            s_copy(r, other(i), me).wait_send()

        loop(1, n, leave_out)


def shards(queries, new_k, new_v, cache_k, cache_v, cache_len):
    requests, local_rows, q_heads, head_dim = queries.shape
    slots, heads = cache_k.shape[1:3]
    group = q_heads // heads
    n = lax.axis_size("seq")
    rows = local_rows * group
    padded = -(-local_rows // 16) * 16
    owners = max(w for w in range(1, n + 1) if n % w == 0 and w * rows <= max(512, rows))
    span = max(w for w in range(1, heads + 1) if heads % w == 0 and w * slots <= max(1024, slots))

    q = jnp.transpose(
        queries.reshape(requests, local_rows, heads, group, head_dim), (2, 0, 1, 3, 4)
    ).reshape(heads, requests, rows, head_dim)
    new = jnp.transpose(jnp.stack([new_k, new_v]), (3, 1, 0, 2, 4))
    new = jnp.pad(new, ((0, 0), (0, 0), (0, 0), (0, padded - local_rows), (0, 0)))

    bf16, f32, dma = jnp.bfloat16, jnp.float32, pltpu.SemaphoreType.DMA
    scratch = [
        pltpu.VMEM((heads, requests, slots, head_dim), bf16),
        pltpu.VMEM((heads, requests, slots, head_dim), bf16),
        pltpu.VMEM((slots * heads, head_dim), f32),
        pltpu.VMEM((requests, n, rows, head_dim), bf16),
        pltpu.VMEM((requests, 2, heads, padded, head_dim), bf16),
        pltpu.VMEM((requests, heads, slots, head_dim), bf16),
        pltpu.VMEM((requests, heads, slots, head_dim), bf16),
        pltpu.VMEM((requests, n, rows, head_dim), bf16),
        pltpu.VMEM((requests, n, 8, rows), f32),
        pltpu.VMEM((requests, n, rows, head_dim), bf16),
        pltpu.VMEM((requests, n, 8, rows), f32),
        dma((2 + 2 * requests,)),
        dma((n,)), dma((n,)), dma((heads,)), dma((heads,)),
        dma((requests, heads)), dma((requests, heads)),
        dma((requests, heads)), dma((requests, heads)),
        dma((requests, n)), dma((requests, n)), dma((requests, n)), dma((requests, n)),
    ]
    work = requests * n * rows * heads * slots
    vmem = pl.BlockSpec(memory_space=pltpu.VMEM)
    return pl.pallas_call(
        functools.partial(
            kernel, n, heads, requests, slots, local_rows, group, owners, span),
        out_shape=jax.ShapeDtypeStruct(queries.shape, bf16),
        in_specs=[pl.BlockSpec(memory_space=pltpu.SMEM)] + [vmem] * 4,
        out_specs=vmem,
        scratch_shapes=scratch,
        compiler_params=pltpu.CompilerParams(
            collective_id=0, has_side_effects=True, vmem_limit_bytes=52 * 1024 * 1024),
        cost_estimate=pl.CostEstimate(
            flops=4 * work * head_dim, bytes_accessed=4 * cache_k.size, transcendentals=work),
    )(cache_len, q, new, cache_k, cache_v)


def solution(mesh):
    spec = P("groups", "seq", None, None)
    in_specs = (spec, spec, spec, spec, spec, P("groups"))
    return jax.shard_map(
        shards, mesh=mesh, in_specs=in_specs, out_specs=spec, check_vma=False)
```

```python
import functools
import math

import jax
import jax.numpy as jnp
from jax import lax
from jax.experimental import pallas as pl
from jax.experimental.pallas import tpu as pltpu
from jax.sharding import PartitionSpec as P

MESH = pl.DeviceIdType.MESH
LOW = -1e30


def loop(start, stop, body):
    def step(i, carry):
        body(i)
        return carry

    lax.fori_loop(start, stop, step, jnp.int32(0))


def kernel(
    n, heads, requests, slots, local_rows, group, owners, span,
    len_ref, q_ref, new_ref, cache_k_ref, cache_v_ref, out_ref, k_ref, v_ref, wide,
    all_q, all_new, all_k, all_v, part, stat, got, got_stat,
    own_sem, q_send, q_recv, new_send, new_recv, k_send, k_recv, v_send, v_recv,
    o_send, o_recv, s_send, s_recv,
):
    me = lax.axis_index("seq")
    block = me // heads
    my_head = lax.rem(me, heads)
    base = block * heads
    blocks = n // heads
    rows = local_rows * group
    padded = all_new.shape[3]
    head_dim = q_ref.shape[-1]
    factor = math.log2(math.e) / math.sqrt(head_dim)

    def turn(cache_ref, turned_ref, r):
        wide[...] = cache_ref[r].astype(jnp.float32).reshape(slots * heads, head_dim)
        for h in range(heads):
            turned_ref[h, r] = wide[pl.ds(h, slots, stride=heads), :].astype(jnp.bfloat16)

    barrier = pltpu.get_barrier_semaphore()
    loop(1, n, lambda i: pl.semaphore_signal(
        barrier, inc=1, device_id={"seq": lax.rem(me + i, n)}, device_id_type=MESH))
    turn(cache_k_ref, k_ref, 0)
    pl.semaphore_wait(barrier, n - 1)

    def remote(src, dst, send, recv, device):
        return pltpu.make_async_remote_copy(
            src_ref=src, dst_ref=dst, send_sem=send, recv_sem=recv,
            device_id={"seq": device}, device_id_type=MESH)

    def q_copy(device, source):
        return remote(q_ref.at[lax.rem(device, heads)], all_q.at[:, source],
                      q_send.at[device], q_recv.at[source], device)

    def new_copy(j, source):
        return remote(new_ref.at[j], all_new.at[:, :, source],
                      new_send.at[j], new_recv.at[source], base + j)

    def k_copy(r, j, source):
        return remote(k_ref.at[j, r], all_k.at[r, source],
                      k_send.at[r, j], k_recv.at[r, source], base + j)

    def v_copy(r, j, source):
        return remote(v_ref.at[j, r], all_v.at[r, source],
                      v_send.at[r, j], v_recv.at[r, source], base + j)

    def o_copy(r, device, source):
        return remote(part.at[r, device], got.at[r, source],
                      o_send.at[r, device], o_recv.at[r, source], device)

    def s_copy(r, device, source):
        return remote(stat.at[r, device], got_stat.at[r, source],
                      s_send.at[r, device], s_recv.at[r, source], device)

    other = lambda i: lax.rem(me + i, n)
    peer = lambda i: lax.rem(my_head + i, heads)

    loop(1, n, lambda i: q_copy(other(i), me).start())
    loop(1, heads, lambda i: new_copy(peer(i), my_head).start())
    for r in range(requests):
        if r > 0:
            turn(cache_k_ref, k_ref, r)
        loop(1, heads, lambda i: k_copy(r, peer(i), my_head).start())
        turn(cache_v_ref, v_ref, r)
        loop(1, heads, lambda i: v_copy(r, peer(i), my_head).start())

    own = [
        pltpu.make_async_copy(q_ref.at[my_head], all_q.at[:, me], own_sem.at[0]),
        pltpu.make_async_copy(new_ref.at[my_head], all_new.at[:, :, my_head], own_sem.at[1]),
    ]
    for r in range(requests):
        own.append(pltpu.make_async_copy(
            k_ref.at[my_head, r], all_k.at[r, my_head], own_sem.at[2 + 2 * r]))
        own.append(pltpu.make_async_copy(
            v_ref.at[my_head, r], all_v.at[r, my_head], own_sem.at[3 + 2 * r]))
    for copy in own:
        copy.start()
    for copy in own:
        copy.wait()

    loop(1, n, lambda i: q_copy(me, other(i)).wait_recv())
    loop(1, heads, lambda i: new_copy(my_head, peer(i)).wait_recv())

    step_rows = owners * rows
    steps = n // owners
    for r in range(requests):
        loop(1, heads, lambda i: k_copy(r, my_head, peer(i)).wait_recv())
        loop(1, heads, lambda i: v_copy(r, my_head, peer(i)).wait_recv())
        filled = len_ref[r]

        def attend(i, r=r, filled=filled):
            step = lax.rem(i + me, steps)
            first = step * owners
            q = all_q[r, pl.ds(first, owners)].reshape(step_rows, head_dim)

            def absorb(state, scores, values):
                peak, total, value = state
                new_peak = jnp.maximum(peak, jnp.max(scores, axis=1, keepdims=True))
                rescale = jnp.exp2(peak - new_peak)
                weights = jnp.exp2(scores - new_peak)
                total = total * rescale + jnp.sum(weights, axis=1, keepdims=True)
                value = value * rescale + jnp.dot(
                    weights.astype(jnp.bfloat16), values, preferred_element_type=jnp.float32)
                return new_peak, total, value

            def score(keys):
                return lax.dot_general(
                    q, keys, (((1,), (1,)), ((), ())),
                    preferred_element_type=jnp.float32) * factor

            state = (
                jnp.full((step_rows, 1), LOW, jnp.float32),
                jnp.zeros((step_rows, 1), jnp.float32),
                jnp.zeros((step_rows, head_dim), jnp.float32),
            )
            for c in range(0, heads, span):
                keys = all_k[r, c:c + span].reshape(span * slots, head_dim)
                values = all_v[r, c:c + span].reshape(span * slots, head_dim)
                pos = (base + c) * slots + lax.broadcasted_iota(
                    jnp.int32, (1, span * slots), 1)
                bias = jnp.where(pos < filled, 0.0, LOW)
                state = absorb(state, score(keys) + bias, values)
            width = heads * padded
            keys = all_new[r, 0].reshape(width, head_dim)
            values = all_new[r, 1].reshape(width, head_dim)
            lane = lax.broadcasted_iota(jnp.int32, (step_rows, width), 1)
            row = lax.broadcasted_iota(jnp.int32, (step_rows, width), 0)
            inner = lax.rem(lane, padded)
            key_pos = (base + lax.div(lane, padded)) * local_rows + inner
            row_pos = first * local_rows + lax.div(row, group)
            valid = (inner < local_rows) & (key_pos <= row_pos)
            peak, total, value = absorb(
                state, jnp.where(valid, score(keys), LOW), values)

            result = (value * (1.0 / total)).astype(jnp.bfloat16).reshape(owners, rows, head_dim)
            lanes = lax.broadcasted_iota(jnp.int32, (step_rows, 128), 1)
            turned = jnp.where(lanes == 0, peak, total).T[:8]
            part[r, pl.ds(first, owners)] = result
            for j in range(owners):
                stat[r, first + j] = turned[:, j * rows:(j + 1) * rows]
            for j in range(owners):
                owner = first + j

                @pl.when(owner != me)
                def _():
                    o_copy(r, owner, me).start()
                    s_copy(r, owner, me).start()

                @pl.when(owner == me)
                def _():
                    got[r, owner] = result[j]
                    got_stat[r, owner] = turned[:, j * rows:(j + 1) * rows]

        loop(0, steps, attend)

    for r in range(requests):
        def arrive(i, r=r):
            o_copy(r, me, other(i)).wait_recv()
            s_copy(r, me, other(i)).wait_recv()

        loop(1, n, arrive)

        stats = [got_stat[r, b * heads:(b + 1) * heads] for b in range(blocks)]
        top = functools.reduce(jnp.maximum, [s[:, 0] for s in stats])
        shares = [s[:, 1] * jnp.exp2(s[:, 0] - top) for s in stats]
        whole = functools.reduce(jnp.add, shares)
        shares = [s / whole for s in shares]
        fill = -n % 128
        if fill:
            shares.append(jnp.zeros((fill, rows), jnp.float32))
        shares = jnp.concatenate(shares, axis=0).T
        for k in range(heads):
            merged = functools.reduce(jnp.add, [
                shares[:, b * heads + k:b * heads + k + 1]
                * got[r, b * heads + k].astype(jnp.float32)
                for b in range(blocks)])
            merged = merged.astype(jnp.bfloat16).reshape(local_rows, group, head_dim)
            out_ref[r, :, k * group:(k + 1) * group, :] = merged

    loop(1, n, lambda i: q_copy(other(i), me).wait_send())
    loop(1, heads, lambda i: new_copy(peer(i), my_head).wait_send())
    for r in range(requests):
        def leave(i, r=r):
            k_copy(r, peer(i), my_head).wait_send()
            v_copy(r, peer(i), my_head).wait_send()

        loop(1, heads, leave)

        def leave_out(i, r=r):
            o_copy(r, other(i), me).wait_send()
            s_copy(r, other(i), me).wait_send()

        loop(1, n, leave_out)


def shards(queries, new_k, new_v, cache_k, cache_v, cache_len):
    requests, local_rows, q_heads, head_dim = queries.shape
    slots, heads = cache_k.shape[1:3]
    group = q_heads // heads
    n = lax.axis_size("seq")
    rows = local_rows * group
    padded = -(-local_rows // 16) * 16
    owners = max(w for w in range(1, n + 1) if n % w == 0 and w * rows <= max(512, rows))
    span = max(w for w in range(1, heads + 1) if heads % w == 0 and w * slots <= max(1024, slots))

    q = jnp.transpose(
        queries.reshape(requests, local_rows, heads, group, head_dim), (2, 0, 1, 3, 4)
    ).reshape(heads, requests, rows, head_dim)
    new = jnp.transpose(jnp.stack([new_k, new_v]), (3, 1, 0, 2, 4))
    new = jnp.pad(new, ((0, 0), (0, 0), (0, 0), (0, padded - local_rows), (0, 0)))

    bf16, f32, dma = jnp.bfloat16, jnp.float32, pltpu.SemaphoreType.DMA
    scratch = [
        pltpu.VMEM((heads, requests, slots, head_dim), bf16),
        pltpu.VMEM((heads, requests, slots, head_dim), bf16),
        pltpu.VMEM((slots * heads, head_dim), f32),
        pltpu.VMEM((requests, n, rows, head_dim), bf16),
        pltpu.VMEM((requests, 2, heads, padded, head_dim), bf16),
        pltpu.VMEM((requests, heads, slots, head_dim), bf16),
        pltpu.VMEM((requests, heads, slots, head_dim), bf16),
        pltpu.VMEM((requests, n, rows, head_dim), bf16),
        pltpu.VMEM((requests, n, 8, rows), f32),
        pltpu.VMEM((requests, n, rows, head_dim), bf16),
        pltpu.VMEM((requests, n, 8, rows), f32),
        dma((2 + 2 * requests,)),
        dma((n,)), dma((n,)), dma((heads,)), dma((heads,)),
        dma((requests, heads)), dma((requests, heads)),
        dma((requests, heads)), dma((requests, heads)),
        dma((requests, n)), dma((requests, n)), dma((requests, n)), dma((requests, n)),
    ]
    work = requests * n * rows * heads * slots
    vmem = pl.BlockSpec(memory_space=pltpu.VMEM)
    return pl.pallas_call(
        functools.partial(
            kernel, n, heads, requests, slots, local_rows, group, owners, span),
        out_shape=jax.ShapeDtypeStruct(queries.shape, bf16),
        in_specs=[pl.BlockSpec(memory_space=pltpu.SMEM)] + [vmem] * 4,
        out_specs=vmem,
        scratch_shapes=scratch,
        compiler_params=pltpu.CompilerParams(
            collective_id=0, has_side_effects=True, vmem_limit_bytes=52 * 1024 * 1024),
        cost_estimate=pl.CostEstimate(
            flops=4 * work * head_dim, bytes_accessed=4 * cache_k.size, transcendentals=work),
    )(cache_len, q, new, cache_k, cache_v)


def solution(mesh):
    spec = P("groups", "seq", None, None)
    in_specs = (spec, spec, spec, spec, spec, P("groups"))
    return jax.shard_map(
        shards, mesh=mesh, in_specs=in_specs, out_specs=spec, check_vma=False)
```
